32 devices in a mesh: groups: 2 (over x), seq: 16 (over z, y, core).
Axes of the slice: x: 2, y: 2, z: 4, core: 2. Of those that a mesh axis runs over, the one named last changes fastest.
Arguments:
- queries: bfloat16 [4096, 2048], P(('groups', 'seq')), parts along dimension 0, may hold values from -6 to 6
- keys: bfloat16 [4096, 1024], P(('groups', 'seq')), parts along dimension 0, may hold values from -6 to 6
- target_rows: bfloat16 [512, 2048], replicated, may hold values from -6 to 6
- target_ids: int32 [4096, 4], P(('groups', 'seq')), parts along dimension 0, may hold values from 0 to 511
- target_weight: float32 [4096, 4], P(('groups', 'seq')), parts along dimension 0, may hold values from -3 to 3
- block_mask: int32 [32, 7], P(('groups', 'seq')), parts along dimension 0, may hold values 0 or 1
- value_table: bfloat16 [1024, 1024], P('seq'), may hold values from -0.75 to 0.75
- feat_shard: int32 [4096, 8], P(('groups', 'seq')), parts along dimension 0, may hold values from 0 to 15, all different within a row; in each aligned block of 128 rows (0 to 127, 128 to 255, ...) at most 96 rows name the same one
- feat_row: int32 [4096, 8], P(('groups', 'seq')), parts along dimension 0, may hold values from 0 to 63
- activation: float32 [4096, 8], P(('groups', 'seq')), parts along dimension 0, may hold values from 0.2 to 5
- counts: int32 [4096], P(('groups', 'seq')), parts along dimension 0, may hold values from 1 to 8, 12288 in all
Outputs:
- value_grad: bfloat16 [4096, 1024], P(('groups', 'seq')), parts along dimension 0
- edges: float32 [4096, 8], P(('groups', 'seq')), parts along dimension 0
The draws below stay inside these ranges and needn't reach their ends.
There are 2 independent parts, one for each index of `groups`. The reference program is written for one: setup_inputs(seed, part) draws one part's arguments, and reference() takes and returns one part's arrays. A program takes and returns all parts, laid end to end along the dimension named above; an argument that names none is the same for every part. Nothing has to cross between parts.
Inputs may be any that keep to these rules, and one draw needn't show every extreme that they name: `feat_shard`: the 8 shards named by one token are different; among the tokens of one block no shard is named by more than 96 slots, a bound that some block reaches. The counts of a prompt sum to 12288.
All inputs are finite; a program needn't handle non-finite values. No bound on the sum of `block_mask` or of `counts` on one device may be relied on, other than what follows from the above.
Results may differ from the reference program's by a relative error of at most 0.0085.
Values may be sent and summed in bfloat16 or wider, within the bound.
A program may use at most 128 MiB of HBM per device.

```python
import math
import jax
import jax.numpy as jnp
import numpy as np
from jax import lax

H = 16
KVH = 8
HD = 128
QPRE = 144
WB = 8
TOK_DEV = 128
NTGT = 512
TPT = 4
ACTIVE = 8
FEAT_DEV = 64
FEATS = 1024
TOKENS = 2048
NB = 16
CAP = 96
N_SEQ = 16


def place_ends(result, own_key, low, high):
    extent = result.shape
    place = [jax.random.randint(jax.random.fold_in(own_key, axis), (), 0, extent[axis]) for axis in range(len(extent))]
    result = result.at[tuple(place)].set(low)
    longest = extent.index(max(extent))
    place[longest] = (place[longest] + 1) % extent[longest]
    return result.at[tuple(place)].set(high)


def steps_of(key, extent, cuts, least, high):
    def one(dim, parts):
        heights = jax.random.uniform(jax.random.fold_in(jax.random.fold_in(key, 6), dim), (parts,), jnp.float32, least / len(cuts), high / len(cuts))
        return jnp.repeat(jnp.exp(heights), extent[dim] // parts).reshape((-1,) + (1,) * (len(extent) - dim - 1))

    factor_of = one(*cuts[0])
    for cut in cuts[1:]:
        factor_of = factor_of * one(*cut)
    return factor_of


def rank_table(count, slope):
    loads = [(1 << 20) // math.isqrt(standing ** slope) + 1 for standing in range(1, count + 1)]
    deviation = 1 + sum(loads) // (1 << 30)
    return np.cumsum(np.array([max(1, weight // deviation) for weight in loads]))


def ranked_ids(own_key, extent, number_of, lean):
    table = rank_table(number_of, lean)
    lot = jax.random.randint(jax.random.fold_in(own_key, 1), extent, 0, int(table[number_of - 1]))
    rank = jnp.searchsorted(jnp.asarray(table, jnp.int32), lot, side="right")
    return jax.random.permutation(jax.random.fold_in(own_key, 2), number_of)[rank].astype(jnp.int32)


def length_profile(number_of, total, reach, lean):
    loads = [(1 << 20) // math.isqrt(grade ** lean) + 1 for grade in range(2, number_of + 1)]
    surplus, given = total - reach - (number_of - 1), [1] * (number_of - 1)
    while surplus > 0:
        candidates = [i for i in range(number_of - 1) if given[i] < reach]
        pool, budget = sum([loads[i] for i in candidates]), surplus
        for i in candidates:
            extra = min(reach - given[i], max(1, budget * loads[i] // pool), surplus)
            given[i] = given[i] + extra
            surplus = surplus - extra
    return np.array([reach] + given)


def uneven_parts(stream_key, amount, total, reach, slope):
    if amount == 2:
        one = jax.random.randint(stream_key, (), max(1, total - reach), min(reach, total - 1) + 1)
        return jnp.stack([one, total - one])
    sizes = jnp.asarray(length_profile(amount, total, reach, slope), jnp.int32)
    pairs = (amount - 1) // 2
    donor, receiver = sizes[1:1 + 2 * pairs:2], sizes[2:2 + 2 * pairs:2]
    slack = jnp.minimum(donor - 1, reach - receiver)
    moved = jax.random.randint(jax.random.fold_in(stream_key, 1), (pairs,), 0, 1 << 20) % (slack + 1)
    sizes = sizes.at[1:1 + 2 * pairs:2].set(donor - moved).at[2:2 + 2 * pairs:2].set(receiver + moved)
    return sizes[jax.random.permutation(jax.random.fold_in(stream_key, 2), amount)]


def deal_out(own_key, own, number, rows, count, top, most, lean):
    order = jax.random.permutation(own_key, count)
    packed, common = shares(count, rows * top, most, lean, True), shares(count, rows * top, most, lean, False)
    places = jnp.arange(count)

    def named(lengths, offset_by):
        used = int((lengths > 0).sum())
        fixed = max(1, used // 4)
        moved = fixed + (places - fixed + offset_by * (used - fixed)) % max(1, count - fixed)
        return jnp.zeros((count,), jnp.int32).at[order[jnp.where(places < fixed, places, moved)]].set(jnp.asarray(lengths, jnp.int32))

    lengths = jnp.where(number % 4 == 0, named(packed, number // 4), named(common, number - number // 4 - 1))
    mixed = jax.random.permutation(jax.random.fold_in(own, 3), count)
    donor, taker = mixed[0:count // 2 * 2:2], mixed[1:count // 2 * 2:2]
    margin = jnp.minimum(lengths[donor] - 1, most - lengths[taker]) // 2
    margin = jnp.where((donor == order[0]) | (taker == order[0]) | (lengths[taker] == 0), 0, jnp.maximum(margin, 0))
    moved = jax.random.randint(jax.random.fold_in(own, 4), (count // 2,), 0, 1 << 20) % (margin + 1)
    lengths = lengths.at[donor].add(-moved).at[taker].add(moved)
    items = jnp.searchsorted(jnp.cumsum(lengths), jnp.arange(rows * top), side="right").astype(jnp.int32)
    listing = items.reshape(top, rows).T
    listing = listing[jax.random.permutation(jax.random.fold_in(own, 1), rows)]
    offset_by = jax.random.randint(jax.random.fold_in(own, 2), (rows, 1), 0, top)
    return jnp.take_along_axis(listing, (jnp.arange(top)[None, :] + offset_by) % top, axis=1)


def shares(amount, total, limit, lean, full):
    weights = [(1 << 20) // math.isqrt(standing ** lean) + 1 for standing in range(1, amount + 1)]
    largest = limit if full else min(limit, max(-(-total // amount), total * weights[0] // sum(weights)))
    least = 1 if total - largest >= amount - 1 else 0
    given, spare = [largest] + [least] * (amount - 1), total - largest - least * (amount - 1)
    while spare > 0:
        free = [i for i in range(1, amount) if given[i] < largest] or [i for i in range(1, amount) if given[i] < limit]
        pool, remaining = sum([weights[i] for i in free]), spare
        for i in free:
            extra = min(limit - given[i], max(1, remaining * weights[i] // pool), spare)
            given[i] = given[i] + extra
            spare = spare - extra
    return np.array(given)


def scatter_about(key, extent, spread, reach, shards=(), kind=jnp.bfloat16):
    entries = jax.random.normal(key, extent, jnp.float32) * spread
    if len(shards) > 0:
        entries = steps_of(key, extent, shards, -0.22, 0.18) * entries
    return jnp.clip(entries, min=-reach, max=reach).astype(kind)


def setup_inputs(seed: int = 0, part: int = 0) -> dict:
    seeds = jax.random.split(jax.random.key(seed), 12)
    part_splits = jax.random.split(jax.random.fold_in(seeds[11], part), 12)
    queries = scatter_about(part_splits[0], (TOKENS, H * HD), 1.0, 6.0, ((0, 16),))
    keys = scatter_about(part_splits[1], (TOKENS, KVH * HD), 1.0, 6.0, ((0, 16),))
    target_rows = scatter_about(seeds[2], (NTGT, H * HD), 1.0, 6.0)
    target_ids = place_ends(jax.random.randint(part_splits[3], (TOKENS, TPT), 0, NTGT), jax.random.fold_in(part_splits[3], 1), 0, NTGT - 1).astype(jnp.int32)
    target_weight = scatter_about(part_splits[4], (TOKENS, TPT), 0.5, 3.0, ((0, 16),), jnp.float32)
    block_mask = place_ends((jax.random.randint(part_splits[5], (NB, WB - 1), 0, 2) < 1).astype(jnp.int32), jax.random.fold_in(part_splits[5], 1), 0, 1)
    value_table = scatter_about(seeds[6], (FEATS, KVH * HD), (KVH * HD // 16) ** -0.5, 0.75, ((0, 16),))
    feat_shard_keys = jax.random.split(jax.random.fold_in(part_splits[7], 1), TOKENS // TOK_DEV)
    feat_shard_turns = jax.random.permutation(jax.random.fold_in(part_splits[7], 3), TOKENS // TOK_DEV)
    feat_shard = jax.vmap(lambda own, number: deal_out(jax.random.fold_in(part_splits[7], 2), own, number, TOK_DEV, N_SEQ, ACTIVE, CAP, 2))(feat_shard_keys, feat_shard_turns).reshape((TOKENS, ACTIVE))
    feat_row = place_ends(ranked_ids(part_splits[8], (TOKENS, ACTIVE), FEAT_DEV, 2), jax.random.fold_in(part_splits[8], 3), 0, FEAT_DEV - 1).astype(jnp.int32)
    activation = jnp.clip(jnp.exp(math.log(5.0) - 3.218876 * jax.random.uniform(part_splits[9], (TOKENS, ACTIVE), jnp.float32) ** steps_of(part_splits[9], (TOKENS, ACTIVE), ((0, 16),), -0.2, 0.2)), 0.2, 5.0)
    counts = uneven_parts(part_splits[10], TOKENS, TOKENS * ACTIVE * 3 // 4, ACTIVE, 0).astype(jnp.int32)
    return {"queries": queries, "keys": keys, "target_rows": target_rows, "target_ids": target_ids, "target_weight": target_weight, "block_mask": block_mask, "value_table": value_table, "feat_shard": feat_shard, "feat_row": feat_row, "activation": activation, "counts": counts}


SOFTCAP = 50.0


def reference(queries, keys, target_rows, target_ids, target_weight, block_mask, value_table, feat_shard, feat_row, activation, counts):
    tok_rows = TOK_DEV
    head_group = H // KVH
    kv_width = KVH * HD
    padded_keys = jnp.concatenate([jnp.zeros(((WB - 1) * tok_rows, kv_width), jnp.bfloat16), keys], axis=0)
    lower_tri = jnp.arange(tok_rows)[:, None] >= jnp.arange(tok_rows)[None, :]
    distance = (WB - 1 - jnp.arange(WB)).astype(jnp.int32)

    def one_block(grad_pad, block):
        start = (block * tok_rows).astype(jnp.int32)
        query = lax.dynamic_slice_in_dim(queries, start, tok_rows, 0).astype(jnp.float32).reshape(tok_rows, KVH, head_group, HD)
        picked = lax.dynamic_slice_in_dim(target_ids, start, tok_rows, 0)
        scaled = lax.dynamic_slice_in_dim(target_weight, start, tok_rows, 0)
        head_grad = jnp.sum(scaled[:, :, None] * target_rows[picked].astype(jnp.float32), axis=1).astype(jnp.bfloat16)
        window = lax.dynamic_slice_in_dim(padded_keys, start, WB * tok_rows, 0).astype(jnp.float32).reshape(WB, tok_rows, KVH, HD)
        logits = jnp.einsum('qhgd,wkhd->whgqk', query, window) * (QPRE ** -0.5)
        logits = SOFTCAP * jnp.tanh(logits / SOFTCAP)
        mask_row = lax.dynamic_slice_in_dim(block_mask, block.astype(jnp.int32), 1, 0)[0]
        mask_full = jnp.concatenate([jnp.ones((1,), jnp.int32), mask_row])
        tile_ok = jnp.where(distance == 0, True, (mask_full[distance] == 1) & (block >= distance))
        keep = tile_ok[:, None, None, None, None] & jnp.where((distance == 0)[:, None, None, None, None], lower_tri[None, None, None], True)
        weights = jnp.where(keep, jnp.exp(logits), 0.0)
        totals = jnp.sum(weights, axis=(0, 4))
        pattern = (weights / totals[None, :, :, :, None]).astype(jnp.bfloat16)
        head_grads = head_grad.astype(jnp.float32).reshape(tok_rows, KVH, head_group, HD)
        part = jnp.einsum('whgqk,qhgd->wkhd', pattern.astype(jnp.float32), head_grads).reshape(WB * tok_rows, kv_width)
        current = lax.dynamic_slice_in_dim(grad_pad, start, WB * tok_rows, 0)
        grad_pad = lax.dynamic_update_slice_in_dim(grad_pad, current + part, start, 0)
        return grad_pad, None

    grad_pad, _ = lax.scan(one_block, jnp.zeros(((NB + WB - 1) * tok_rows, kv_width), jnp.float32), jnp.arange(NB, dtype=jnp.int32))
    value_grad = grad_pad[(WB - 1) * tok_rows:].astype(jnp.bfloat16)
    feature = feat_shard * FEAT_DEV + feat_row

    def edge_block(pieces):
        grads, ids, acts, lives = pieces
        rows = value_table[ids].astype(jnp.float32)
        raw = jnp.einsum('tw,taw->ta', grads.astype(jnp.float32), rows)
        live = jnp.arange(ACTIVE)[None, :] < lives[:, None]
        return jnp.where(live, acts * raw, 0.0)

    edges = lax.map(edge_block, (value_grad.reshape(NB, tok_rows, kv_width), feature.reshape(NB, tok_rows, ACTIVE), activation.reshape(NB, tok_rows, ACTIVE), counts.reshape(NB, tok_rows)))
    return value_grad, edges.reshape(TOKENS, ACTIVE)
```

```python
import functools
import math

import jax
import jax.numpy as jnp
from jax import lax
from jax.experimental import pallas as pl
from jax.experimental.pallas import tpu as pltpu
from jax.sharding import PartitionSpec as P

H = 16
KVH = 8
HD = 128
QPRE = 144
WB = 8
FEAT_DEV = 64
SOFTCAP = 50.0

CHUNKS = 4
GROUP = H // KVH
HEADS = KVH // CHUNKS
REACH = (WB - 2) // 2
ROLES = WB
MESH = pl.DeviceIdType.MESH
VMEM_LIMIT = 48 * 1024 * 1024


def attention_kernel(
    n,
    q_hbm,
    k_ref,
    rows_hbm,
    ids_ref,
    weight_ref,
    mask_ref,
    out_ref,
    q_vm,
    rows_vm,
    kbuf,
    hgrad,
    wbuf,
    acc,
    pown,
    psend,
    psum,
    rsib,
    rgrad,
    load_sem,
    ksend,
    krecv,
    gsend,
    grecv,
):
    tok = k_ref.shape[0]
    width = k_ref.shape[1] // CHUNKS
    b = lax.axis_index("seq")
    core = lax.rem(b, 2)
    chip = lax.div(b, 2)
    chips = n // 2
    sib = b + 1 - 2 * core
    ahead = [chip + d < chips for d in range(1, REACH + 1)]
    behind = [chip >= d for d in range(1, REACH + 1)]
    last_ahead = chip + 4 * core < chips
    last_behind = chip >= 4 * (1 - core)
    last_key_to = b + 1 + 6 * core
    last_grad_to = b - 7 + 6 * core
    far = b - 7 + 14 * core
    has_far = jnp.logical_and(far >= 0, far < n)

    load_q = pltpu.make_async_copy(q_hbm, q_vm, load_sem.at[0])
    load_rows = pltpu.make_async_copy(rows_hbm, rows_vm, load_sem.at[1])
    load_rows.start()
    load_q.start()

    barrier = pltpu.get_barrier_semaphore()
    partners = [(sib, None), (far, has_far)]
    for d in range(1, REACH + 1):
        partners.append((b + 2 * d, ahead[d - 1]))
        partners.append((b - 2 * d, behind[d - 1]))

    def greet(device):
        pl.semaphore_signal(barrier, inc=1, device_id={"seq": device}, device_id_type=MESH)

    for device, cond in partners:
        if cond is None:
            greet(device)
        else:
            pl.when(cond)(functools.partial(greet, device))
    peers = 1
    for _, cond in partners[1:]:
        peers = peers + jnp.where(cond, 1, 0)
    pl.semaphore_wait(barrier, peers)

    def cols(k):
        return pl.ds(pl.multiple_of(k * width, width), width)

    def remote(src, dst, send, recv, device):
        return pltpu.make_async_remote_copy(
            src_ref=src,
            dst_ref=dst,
            send_sem=send,
            recv_sem=recv,
            device_id={"seq": device},
            device_id_type=MESH,
        )

    def key_direct(d, k, device):
        return remote(
            k_ref.at[:, cols(k)], kbuf.at[d - 1, k], ksend.at[d - 1, k], krecv.at[d - 1, k], device
        )

    def key_share(d, k):
        i = REACH + d - 1
        return remote(kbuf.at[d - 1, k], kbuf.at[i, k], ksend.at[i, k], krecv.at[i, k], sib)

    def key_last(k, device):
        i = 2 * REACH
        return remote(k_ref.at[:, cols(k)], kbuf.at[i, k], ksend.at[i, k], krecv.at[i, k], device)

    def grad_share(d, k):
        return remote(
            psend.at[d - 1, k], rsib.at[d - 1, k], gsend.at[d - 1, k], grecv.at[d - 1, k], sib
        )

    def grad_direct(d, k, device):
        i = REACH + d - 1
        return remote(psum.at[d - 1, k], rgrad.at[d - 1, k], gsend.at[i, k], grecv.at[i, k], device)

    def grad_last(k, device):
        i = 2 * REACH
        return remote(
            psend.at[REACH, k], rgrad.at[REACH, k], gsend.at[i, k], grecv.at[i, k], device
        )

    for k in range(CHUNKS):
        for d in range(1, REACH + 1):
            pl.when(ahead[d - 1])(lambda d=d, k=k: key_direct(d, k, b + 2 * d).start())
        pl.when(last_ahead)(lambda k=k: key_last(k, last_key_to).start())

    load_rows.wait()
    targets = rows_vm.shape[0]
    lane = lax.broadcasted_iota(jnp.int32, (tok, targets), 1)
    spread = jnp.zeros((tok, targets), jnp.float32)
    for j in range(ids_ref.shape[1]):
        spread = spread + jnp.where(lane == ids_ref[:, j : j + 1], weight_ref[:, j : j + 1], 0.0)
    high = spread.astype(jnp.bfloat16)
    low = (spread - high.astype(jnp.float32)).astype(jnp.bfloat16)
    for g in range(KVH):
        part = rows_vm[:, g * GROUP * HD : (g + 1) * GROUP * HD]
        grad = jnp.dot(high, part, preferred_element_type=jnp.float32) + jnp.dot(
            low, part, preferred_element_type=jnp.float32
        )
        grad = grad.astype(jnp.bfloat16)
        for h in range(GROUP):
            hgrad[g, h * tok : (h + 1) * tok, :] = grad[:, h * HD : (h + 1) * HD]
    load_q.wait()

    key_row = lax.broadcasted_iota(jnp.int32, (tok, GROUP * tok), 0)
    tok_col = lax.rem(lax.broadcasted_iota(jnp.int32, (tok, GROUP * tok), 1), tok)
    causal = key_row <= tok_col

    def tile_work(k):
        for gi in range(HEADS):
            mine = slice(gi * HD, (gi + 1) * HD)
            pair = GROUP * HD
            offset = pl.multiple_of(k * (HEADS * pair) + gi * pair, pair)
            q = q_vm[:, pl.ds(offset, pair)]
            q2 = jnp.concatenate([q[:, h * HD : (h + 1) * HD] for h in range(GROUP)], axis=0)
            total = jnp.zeros((1, GROUP * tok), jnp.float32)
            for r in range(ROLES):
                if r == 0:
                    start = pl.multiple_of(k * width + gi * HD, HD)
                    key = k_ref[:, pl.ds(start, HD)]
                    keep = causal
                else:
                    key = kbuf[r - 1, k, :, mine]
                    keep = mask_ref[r : r + 1, :] > 0.5
                score = lax.dot_general(
                    key, q2, (((1,), (1,)), ((), ())), preferred_element_type=jnp.float32
                )
                logit = (SOFTCAP * math.log2(math.e)) * jnp.tanh(
                    score * (QPRE ** (-0.5) / SOFTCAP)
                )
                w = jnp.exp2(jnp.where(keep, logit, -1.0e5))
                wbuf[r] = w
                total = total + jnp.sum(w, axis=0, keepdims=True)
            scale = 1.0 / total
            grad = hgrad[k * HEADS + gi]
            for r in range(ROLES):
                pattern = (wbuf[r] * scale).astype(jnp.bfloat16)
                part = jnp.dot(pattern, grad, preferred_element_type=jnp.float32)
                if r == 0:
                    acc[k, :, mine] = part
                elif r <= REACH:
                    pown[r - 1, k, :, mine] = part
                else:
                    psend[r - 1 - REACH, k, :, mine] = part.astype(jnp.bfloat16)

    def reduce_pair(k):
        for d in range(1, REACH + 1):

            def one(d=d):
                grad_share(d, k).wait_recv()
                both = pown[d - 1, k] + rsib[d - 1, k].astype(jnp.float32)
                psum[d - 1, k] = both.astype(jnp.bfloat16)
                grad_direct(d, k, b - 2 * d).start()

            pl.when(behind[d - 1])(one)

    def chunk(k, carry):
        for d in range(1, REACH + 1):

            def share(d=d):
                key_direct(d, k, sib).wait_recv()
                key_share(d, k).start()

            pl.when(behind[d - 1])(share)
        for d in range(1, REACH + 1):
            pl.when(behind[d - 1])(lambda d=d: key_share(d, k).wait_recv())
        pl.when(last_behind)(lambda: key_last(k, sib).wait_recv())
        tile_work(k)
        for d in range(1, REACH + 1):
            pl.when(behind[d - 1])(lambda d=d: grad_share(d, k).start())
        pl.when(last_behind)(lambda: grad_last(k, last_grad_to).start())
        pl.when(k > 0)(lambda: reduce_pair(k - 1))
        return carry

    lax.fori_loop(0, CHUNKS, chunk, 0)
    reduce_pair(CHUNKS - 1)

    def finish(k, carry):
        for d in range(1, REACH + 1):

            def add(d=d):
                grad_direct(d, k, sib).wait_recv()
                acc[k] += rgrad[d - 1, k].astype(jnp.float32)

            pl.when(ahead[d - 1])(add)

        def add_last():
            grad_last(k, sib).wait_recv()
            acc[k] += rgrad[REACH, k].astype(jnp.float32)

        pl.when(last_ahead)(add_last)
        out_ref[:, cols(k)] = acc[k].astype(out_ref.dtype)
        return carry

    lax.fori_loop(0, CHUNKS, finish, 0)

    def drain(k, carry):
        for d in range(1, REACH + 1):
            pl.when(ahead[d - 1])(lambda d=d: key_direct(d, k, sib).wait_send())

            def back(d=d):
                key_share(d, k).wait_send()
                grad_share(d, k).wait_send()
                grad_direct(d, k, sib).wait_send()

            pl.when(behind[d - 1])(back)
        pl.when(last_ahead)(lambda: key_last(k, sib).wait_send())
        pl.when(last_behind)(lambda: grad_last(k, sib).wait_send())
        return carry

    lax.fori_loop(0, CHUNKS, drain, 0)


def edges_kernel(vg_ref, table_ref, shard_ref, row_ref, act_ref, vg_out, edges_ref, wide):
    tok, slots = shard_ref.shape
    vg = vg_ref[...]
    vg_out[...] = vg
    wide[...] = jnp.zeros_like(wide)
    wide[:, 0:slots] = shard_ref[...] * FEAT_DEV + row_ref[...]
    feature = wide[...]
    tile = lax.div(feature, 128)
    within = lax.rem(feature, 128)
    step = 256

    def piece(i, found):
        rows = table_ref[pl.ds(pl.multiple_of(i * step, step), step), :]
        product = lax.dot_general(
            vg, rows, (((1,), (1,)), ((), ())), preferred_element_type=jnp.float32
        )
        for j in range(step // 128):
            picked = jnp.take_along_axis(product[:, j * 128 : (j + 1) * 128], within, axis=1)
            found = jnp.where(tile == i * (step // 128) + j, picked, found)
        return found

    found = lax.fori_loop(
        0, table_ref.shape[0] // step, piece, jnp.zeros((tok, 128), jnp.float32)
    )
    edges_ref[...] = act_ref[...] * found[:, 0:slots]


def body(
    queries,
    keys,
    target_rows,
    target_ids,
    target_weight,
    block_mask,
    value_table,
    feat_shard,
    feat_row,
    activation,
    counts,
):
    tok = queries.shape[0]
    kv_width = keys.shape[1]
    width = kv_width // CHUNKS
    slots = feat_shard.shape[1]
    n = lax.axis_size("seq")
    position = lax.axis_index("seq")
    table = lax.all_gather(value_table, "seq", axis=0, tiled=True)
    live = jnp.arange(slots)[None, :] < counts[:, None]
    act = jnp.where(live, activation, 0.0)

    core = position % 2
    distances = [jnp.zeros_like(position)]
    distances += [jnp.full_like(position, 2 * d) for d in range(1, REACH + 1)]
    distances += [2 * d - 1 + 2 * core for d in range(1, REACH + 1)]
    distances += [7 - 6 * core]
    distance = jnp.stack(distances)
    kept = jnp.sum(
        jnp.where(distance[:, None] - 1 == jnp.arange(WB - 1)[None, :], block_mask, 0), axis=1
    )
    kept = (kept == 1) & (position >= distance)
    mask = jnp.broadcast_to(kept[:, None], (ROLES, GROUP * tok)).astype(jnp.float32)

    vmem = pl.BlockSpec(memory_space=pltpu.VMEM)
    hbm = pl.BlockSpec(memory_space=pl.ANY)
    value_grad = pl.pallas_call(
        functools.partial(attention_kernel, n),
        out_shape=jax.ShapeDtypeStruct((tok, kv_width), jnp.bfloat16),
        in_specs=[hbm, vmem, hbm, vmem, vmem, vmem],
        out_specs=vmem,
        scratch_shapes=[
            pltpu.VMEM(queries.shape, jnp.bfloat16),
            pltpu.VMEM(target_rows.shape, jnp.bfloat16),
            pltpu.VMEM((ROLES - 1, CHUNKS, tok, width), jnp.bfloat16),
            pltpu.VMEM((KVH, GROUP * tok, HD), jnp.bfloat16),
            pltpu.VMEM((ROLES, tok, GROUP * tok), jnp.float32),
            pltpu.VMEM((CHUNKS, tok, width), jnp.float32),
            pltpu.VMEM((REACH, CHUNKS, tok, width), jnp.float32),
            pltpu.VMEM((REACH + 1, CHUNKS, tok, width), jnp.bfloat16),
            pltpu.VMEM((REACH, CHUNKS, tok, width), jnp.bfloat16),
            pltpu.VMEM((REACH, CHUNKS, tok, width), jnp.bfloat16),
            pltpu.VMEM((REACH + 1, CHUNKS, tok, width), jnp.bfloat16),
            pltpu.SemaphoreType.DMA((2,)),
            pltpu.SemaphoreType.DMA((ROLES - 1, CHUNKS)),
            pltpu.SemaphoreType.DMA((ROLES - 1, CHUNKS)),
            pltpu.SemaphoreType.DMA((ROLES - 1, CHUNKS)),
            pltpu.SemaphoreType.DMA((ROLES - 1, CHUNKS)),
        ],
        compiler_params=pltpu.CompilerParams(
            collective_id=0, has_side_effects=True, vmem_limit_bytes=VMEM_LIMIT
        ),
        cost_estimate=pl.CostEstimate(
            flops=2_000_000_000, bytes_accessed=100_000_000, transcendentals=4_000_000
        ),
        name="attention",
    )(queries, keys, target_rows, target_ids, target_weight, mask)

    return pl.pallas_call(
        edges_kernel,
        out_shape=(
            jax.ShapeDtypeStruct((tok, kv_width), jnp.bfloat16),
            jax.ShapeDtypeStruct((tok, slots), jnp.float32),
        ),
        in_specs=[vmem] * 5,
        out_specs=(vmem, vmem),
        scratch_shapes=[pltpu.VMEM((tok, 128), jnp.int32)],
        compiler_params=pltpu.CompilerParams(vmem_limit_bytes=VMEM_LIMIT),
        name="edges",
    )(value_grad, table, feat_shard, feat_row, act)


def solution(mesh):
    tokens = P(("groups", "seq"), None)
    in_specs = (
        tokens,
        tokens,
        P(),
        tokens,
        tokens,
        tokens,
        P("seq", None),
        tokens,
        tokens,
        tokens,
        P(("groups", "seq")),
    )
    return jax.shard_map(
        body, mesh=mesh, in_specs=in_specs, out_specs=(tokens, tokens), check_vma=False
    )
```

```python
import functools
import math

import jax
import jax.numpy as jnp
from jax import lax
from jax.experimental import pallas as pl
from jax.experimental.pallas import tpu as pltpu
from jax.sharding import PartitionSpec as P

H = 16
KVH = 8
HD = 128
QPRE = 144
WB = 8
FEAT_DEV = 64
SOFTCAP = 50.0

CHUNKS = 4
GROUP = H // KVH
HEADS = KVH // CHUNKS
REACH = (WB - 2) // 2
ROLES = WB
MESH = pl.DeviceIdType.MESH
VMEM_LIMIT = 60 * 1024 * 1024


def attention_kernel(
    n,
    q_hbm,
    k_ref,
    rows_hbm,
    ids_ref,
    weight_ref,
    blocks_ref,
    table_hbm,
    shard_ref,
    row_ref,
    act_ref,
    counts_ref,
    out_ref,
    edges_ref,
    mask_ref,
    table_vm,
    q_vm,
    rows_vm,
    kbuf,
    hgrad,
    wbuf,
    acc,
    pown,
    psend,
    psum,
    rsib,
    rgrad,
    load_sem,
    ksend,
    krecv,
    gsend,
    grecv,
    tsend,
    trecv,
):
    tok = k_ref.shape[0]
    width = k_ref.shape[1] // CHUNKS
    b = lax.axis_index("seq")
    core = lax.rem(b, 2)
    chip = lax.div(b, 2)
    chips = n // 2
    sib = b + 1 - 2 * core
    ahead = [chip + d < chips for d in range(1, REACH + 1)]
    behind = [chip >= d for d in range(1, REACH + 1)]
    last_ahead = chip + 4 * core < chips
    last_behind = chip >= 4 * (1 - core)
    last_key_to = b + 1 + 6 * core
    last_grad_to = b - 7 + 6 * core
    far = b - 7 + 14 * core
    has_far = jnp.logical_and(far >= 0, far < n)

    group = lax.axis_index("groups")
    lines = n // 4
    hi = lax.div(b, 4)
    lo = lax.rem(chip, 2)
    mine = core * 2 + lo
    half = table_hbm.shape[0] // 2
    part = pl.ds(pl.multiple_of(group * half, half), half)
    load_table = pltpu.make_async_copy(
        table_hbm.at[part], table_vm.at[mine, hi, part], load_sem.at[2]
    )
    load_table.start()
    load_q = pltpu.make_async_copy(q_hbm, q_vm, load_sem.at[0])
    load_rows = pltpu.make_async_copy(rows_hbm, rows_vm, load_sem.at[1])
    load_rows.start()
    load_q.start()

    barrier = pltpu.get_barrier_semaphore()
    partners = [(sib, None), (far, has_far)]
    for d in (1, 3):
        partners.append((b + 2 * d, ahead[d - 1]))
        partners.append((b - 2 * d, behind[d - 1]))

    def greet(device):
        pl.semaphore_signal(barrier, inc=1, device_id={"seq": device}, device_id_type=MESH)

    def on_line(o):
        return 4 * lax.rem(hi + o, lines) + 2 * lo + core

    for o in range(1, lines):
        greet(on_line(o))
    pl.semaphore_signal(barrier, inc=1, device_id={"groups": 1 - group}, device_id_type=MESH)

    for device, cond in partners:
        if cond is None:
            greet(device)
        else:
            pl.when(cond)(functools.partial(greet, device))
    peers = 1 + lines
    for _, cond in partners[1:]:
        peers = peers + jnp.where(cond, 1, 0)
    pl.semaphore_wait(barrier, peers)

    def cols(k):
        return pl.ds(pl.multiple_of(k * width, width), width)

    def remote(src, dst, send, recv, device):
        return pltpu.make_async_remote_copy(
            src_ref=src,
            dst_ref=dst,
            send_sem=send,
            recv_sem=recv,
            device_id={"seq": device},
            device_id_type=MESH,
        )

    def key_direct(d, k, device):
        return remote(
            k_ref.at[:, cols(k)], kbuf.at[d - 1, k], ksend.at[d - 1, k], krecv.at[d - 1, k], device
        )

    def key_share(d, k):
        i = REACH + d - 1
        return remote(kbuf.at[d - 1, k], kbuf.at[i, k], ksend.at[i, k], krecv.at[i, k], sib)

    def key_last(k, device):
        i = 2 * REACH
        return remote(k_ref.at[:, cols(k)], kbuf.at[i, k], ksend.at[i, k], krecv.at[i, k], device)

    def grad_share(d, k):
        return remote(
            psend.at[d - 1, k], rsib.at[d - 1, k], gsend.at[d - 1, k], grecv.at[d - 1, k], sib
        )

    def grad_direct(d, k, device):
        i = REACH + d - 1
        return remote(psum.at[d - 1, k], rgrad.at[d - 1, k], gsend.at[i, k], grecv.at[i, k], device)

    def grad_last(k, device):
        i = 2 * REACH
        return remote(
            psend.at[REACH, k], rgrad.at[REACH, k], gsend.at[i, k], grecv.at[i, k], device
        )

    def table_line(o):
        piece = table_vm.at[mine, hi, part]
        return remote(piece, piece, tsend.at[o - 1], trecv.at[o - 1], on_line(o))

    def table_lo():
        piece = table_vm.at[mine, :, part]
        i = lines - 1
        return remote(piece, piece, tsend.at[i], trecv.at[i], b + 2 - 4 * lo)

    def table_group():
        piece = table_vm.at[pl.ds(core * 2, 2), :, part]
        i = lines
        return pltpu.make_async_remote_copy(
            src_ref=piece,
            dst_ref=piece,
            send_sem=tsend.at[i],
            recv_sem=trecv.at[i],
            device_id={"groups": 1 - group},
            device_id_type=MESH,
        )

    def table_core():
        piece = table_vm.at[pl.ds(core * 2, 2)]
        i = lines + 1
        return remote(piece, piece, tsend.at[i], trecv.at[i], sib)

    for k in range(CHUNKS):
        for d in range(1, REACH + 1):
            pl.when(ahead[d - 1])(lambda d=d, k=k: key_direct(d, k, b + 2 * d).start())
        pl.when(last_ahead)(lambda k=k: key_last(k, last_key_to).start())

    load_table.wait()
    for o in range(1, lines):
        table_line(o).start()

    load_rows.wait()
    targets = rows_vm.shape[0]
    target = lax.broadcasted_iota(jnp.int32, (targets, tok), 0)
    spread = jnp.zeros((targets, tok), jnp.float32)
    for j in range(ids_ref.shape[0]):
        spread = spread + jnp.where(target == ids_ref[j : j + 1, :], weight_ref[j : j + 1, :], 0.0)
    spread = spread.T
    high = spread.astype(jnp.bfloat16)
    low = (spread - high.astype(jnp.float32)).astype(jnp.bfloat16)
    for g in range(KVH):
        columns = rows_vm[:, g * GROUP * HD : (g + 1) * GROUP * HD]
        grad = jnp.dot(high, columns, preferred_element_type=jnp.float32) + jnp.dot(
            low, columns, preferred_element_type=jnp.float32
        )
        grad = grad.astype(jnp.bfloat16)
        for h in range(GROUP):
            hgrad[g, h * tok : (h + 1) * tok, :] = grad[:, h * HD : (h + 1) * HD]
    load_q.wait()

    def keeps(distance):
        return blocks_ref[0:1, distance - 1 : distance]

    for r in range(1, ROLES):
        if r <= REACH:
            kept, there = keeps(2 * r), behind[r - 1]
        elif r <= 2 * REACH:
            d = r - REACH
            kept = jnp.where(core == 0, keeps(2 * d - 1), keeps(2 * d + 1))
            there = behind[d - 1]
        else:
            kept, there = jnp.where(core == 0, keeps(WB - 1), keeps(1)), last_behind
        kept = jnp.where(there, kept, 0).astype(jnp.float32)
        mask_ref[r : r + 1, :] = jnp.broadcast_to(kept, (1, GROUP * tok))

    key_row = lax.broadcasted_iota(jnp.int32, (tok, GROUP * tok), 0)
    tok_col = lax.rem(lax.broadcasted_iota(jnp.int32, (tok, GROUP * tok), 1), tok)
    causal = key_row <= tok_col

    def tile_work(k):
        for gi in range(HEADS):
            head = slice(gi * HD, (gi + 1) * HD)
            pair = GROUP * HD
            offset = pl.multiple_of(k * (HEADS * pair) + gi * pair, pair)
            q = q_vm[:, pl.ds(offset, pair)]
            q2 = jnp.concatenate([q[:, h * HD : (h + 1) * HD] for h in range(GROUP)], axis=0)
            total = jnp.zeros((1, GROUP * tok), jnp.float32)
            for r in range(ROLES):
                if r == 0:
                    start = pl.multiple_of(k * width + gi * HD, HD)
                    key = k_ref[:, pl.ds(start, HD)]
                    keep = causal
                else:
                    key = kbuf[r - 1, k, :, head]
                    keep = mask_ref[r : r + 1, :] > 0.5
                score = lax.dot_general(
                    key, q2, (((1,), (1,)), ((), ())), preferred_element_type=jnp.float32
                )
                logit = (SOFTCAP * math.log2(math.e)) * jnp.tanh(
                    score * (QPRE ** (-0.5) / SOFTCAP)
                )
                w = jnp.exp2(jnp.where(keep, logit, -1.0e5))
                wbuf[r] = w
                total = total + jnp.sum(w, axis=0, keepdims=True)
            scale = 1.0 / total
            grad = hgrad[k * HEADS + gi]
            for r in range(ROLES):
                pattern = (wbuf[r] * scale).astype(jnp.bfloat16)
                grads = jnp.dot(pattern, grad, preferred_element_type=jnp.float32)
                if r == 0:
                    acc[k, :, head] = grads
                elif r <= REACH:
                    pown[r - 1, k, :, head] = grads
                else:
                    psend[r - 1 - REACH, k, :, head] = grads.astype(jnp.bfloat16)

    def reduce_pair(k):
        for d in range(1, REACH + 1):

            def one(d=d):
                grad_share(d, k).wait_recv()
                both = pown[d - 1, k] + rsib[d - 1, k].astype(jnp.float32)
                psum[d - 1, k] = both.astype(jnp.bfloat16)
                grad_direct(d, k, b - 2 * d).start()

            pl.when(behind[d - 1])(one)

    def chunk(k, carry):
        for d in range(1, REACH + 1):

            def share(d=d):
                key_direct(d, k, sib).wait_recv()
                key_share(d, k).start()

            pl.when(behind[d - 1])(share)
        for d in range(1, REACH + 1):
            pl.when(behind[d - 1])(lambda d=d: key_share(d, k).wait_recv())
        pl.when(last_behind)(lambda: key_last(k, sib).wait_recv())
        tile_work(k)
        for d in range(1, REACH + 1):
            pl.when(behind[d - 1])(lambda d=d: grad_share(d, k).start())
        pl.when(last_behind)(lambda: grad_last(k, last_grad_to).start())
        pl.when(k > 0)(lambda: reduce_pair(k - 1))

        def table_first():
            for o in range(1, lines):
                table_line(o).wait_recv()
            table_lo().start()

        def table_second():
            table_lo().wait_recv()
            table_group().start()

        def table_third():
            table_group().wait_recv()
            table_core().start()

        pl.when(k == 0)(table_first)
        pl.when(k == 1)(table_second)
        pl.when(k == CHUNKS - 1)(table_third)
        return carry

    lax.fori_loop(0, CHUNKS, chunk, 0)
    reduce_pair(CHUNKS - 1)

    def finish(k, carry):
        for d in range(1, REACH + 1):

            def add(d=d):
                grad_direct(d, k, sib).wait_recv()
                acc[k] += rgrad[d - 1, k].astype(jnp.float32)

            pl.when(ahead[d - 1])(add)

        def add_last():
            grad_last(k, sib).wait_recv()
            acc[k] += rgrad[REACH, k].astype(jnp.float32)

        pl.when(last_ahead)(add_last)
        out_ref[:, cols(k)] = acc[k].astype(out_ref.dtype)
        return carry

    lax.fori_loop(0, CHUNKS, finish, 0)

    def drain(k, carry):
        for d in range(1, REACH + 1):
            pl.when(ahead[d - 1])(lambda d=d: key_direct(d, k, sib).wait_send())

            def back(d=d):
                key_share(d, k).wait_send()
                grad_share(d, k).wait_send()
                grad_direct(d, k, sib).wait_send()

            pl.when(behind[d - 1])(back)
        pl.when(last_ahead)(lambda: key_last(k, sib).wait_send())
        pl.when(last_behind)(lambda: grad_last(k, sib).wait_send())
        return carry

    lax.fori_loop(0, CHUNKS, drain, 0)


    table_core().wait_recv()
    shard = shard_ref[...]
    slot = (lax.rem(shard, 2) * 2 + lax.rem(lax.div(shard, 2), 2)) * lines + lax.div(shard, 4)
    depth = table_vm.shape[2]
    feature = slot * depth + row_ref[...]
    slots = feature.shape[0]
    some = math.gcd(lines, 4)
    step = some * depth
    place = lax.broadcasted_iota(jnp.int32, (step, tok), 0)
    vg = out_ref[...]

    def edge_step(i, found):
        per = lines // some
        rows = table_vm[lax.div(i, per), pl.ds(lax.rem(i, per) * some, some)].reshape(step, -1)
        product = lax.dot_general(
            rows, vg, (((1,), (1,)), ((), ())), preferred_element_type=jnp.float32
        )
        local = feature - i * step
        picked = [
            jnp.sum(jnp.where(place == local[a : a + 1, :], product, 0.0), axis=0, keepdims=True)
            for a in range(slots)
        ]
        return found + jnp.concatenate(picked, axis=0)

    found = lax.fori_loop(
        0, 4 * lines // some, edge_step, jnp.zeros((slots, tok), jnp.float32)
    )
    live = lax.broadcasted_iota(jnp.int32, (slots, tok), 0) < counts_ref[...]
    edges_ref[...] = jnp.where(live, act_ref[...] * found, 0.0)

    for o in range(1, lines):
        table_line(o).wait_send()
    table_lo().wait_send()
    table_group().wait_send()
    table_core().wait_send()


def body(
    queries,
    keys,
    target_rows,
    target_ids,
    target_weight,
    block_mask,
    value_table,
    feat_shard,
    feat_row,
    activation,
    counts,
):
    tok = queries.shape[0]
    kv_width = keys.shape[1]
    width = kv_width // CHUNKS
    slots = feat_shard.shape[1]
    n = lax.axis_size("seq")
    lines = n // 4

    vmem = pl.BlockSpec(memory_space=pltpu.VMEM)
    hbm = pl.BlockSpec(memory_space=pl.ANY)
    value_grad, edges = pl.pallas_call(
        functools.partial(attention_kernel, n),
        out_shape=(
            jax.ShapeDtypeStruct((tok, kv_width), jnp.bfloat16),
            jax.ShapeDtypeStruct((slots, tok), jnp.float32),
        ),
        in_specs=[hbm, vmem, hbm, vmem, vmem, vmem, hbm, vmem, vmem, vmem, vmem],
        out_specs=(vmem, vmem),
        scratch_shapes=[
            pltpu.VMEM((ROLES, GROUP * tok), jnp.float32),
            pltpu.VMEM((4, lines) + value_table.shape, jnp.bfloat16),
            pltpu.VMEM(queries.shape, jnp.bfloat16),
            pltpu.VMEM(target_rows.shape, jnp.bfloat16),
            pltpu.VMEM((ROLES - 1, CHUNKS, tok, width), jnp.bfloat16),
            pltpu.VMEM((KVH, GROUP * tok, HD), jnp.bfloat16),
            pltpu.VMEM((ROLES, tok, GROUP * tok), jnp.float32),
            pltpu.VMEM((CHUNKS, tok, width), jnp.float32),
            pltpu.VMEM((REACH, CHUNKS, tok, width), jnp.float32),
            pltpu.VMEM((REACH + 1, CHUNKS, tok, width), jnp.bfloat16),
            pltpu.VMEM((REACH, CHUNKS, tok, width), jnp.bfloat16),
            pltpu.VMEM((REACH, CHUNKS, tok, width), jnp.bfloat16),
            pltpu.VMEM((REACH + 1, CHUNKS, tok, width), jnp.bfloat16),
            pltpu.SemaphoreType.DMA((3,)),
            pltpu.SemaphoreType.DMA((ROLES - 1, CHUNKS)),
            pltpu.SemaphoreType.DMA((ROLES - 1, CHUNKS)),
            pltpu.SemaphoreType.DMA((ROLES - 1, CHUNKS)),
            pltpu.SemaphoreType.DMA((ROLES - 1, CHUNKS)),
            pltpu.SemaphoreType.DMA((lines + 2,)),
            pltpu.SemaphoreType.DMA((lines + 2,)),
        ],
        compiler_params=pltpu.CompilerParams(
            collective_id=0, has_side_effects=True, vmem_limit_bytes=VMEM_LIMIT
        ),
        cost_estimate=pl.CostEstimate(
            flops=2_000_000_000, bytes_accessed=100_000_000, transcendentals=4_000_000
        ),
        name="attention",
    )(
        queries,
        keys,
        target_rows,
        target_ids.T,
        target_weight.T,
        block_mask,
        value_table,
        feat_shard.T,
        feat_row.T,
        activation.T,
        counts[None, :],
    )
    return value_grad, edges.T


def solution(mesh):
    tokens = P(("groups", "seq"), None)
    in_specs = (
        tokens,
        tokens,
        P(),
        tokens,
        tokens,
        tokens,
        P("seq", None),
        tokens,
        tokens,
        tokens,
        P(("groups", "seq")),
    )
    return jax.shard_map(
        body, mesh=mesh, in_specs=in_specs, out_specs=(tokens, tokens), check_vma=False
    )
```

```python
import functools
import math

import jax
import jax.numpy as jnp
from jax import lax
from jax.experimental import pallas as pl
from jax.experimental.pallas import tpu as pltpu
from jax.sharding import PartitionSpec as P

H = 16
KVH = 8
HD = 128
QPRE = 144
WB = 8
FEAT_DEV = 64
SOFTCAP = 50.0

CHUNKS = 4
GROUP = H // KVH
HEADS = KVH // CHUNKS
REACH = (WB - 2) // 2
ROLES = WB
MESH = pl.DeviceIdType.MESH
VMEM_LIMIT = 60 * 1024 * 1024


def attention_kernel(
    n,
    q_hbm,
    k_ref,
    rows_hbm,
    ids_ref,
    weight_ref,
    blocks_ref,
    table_hbm,
    shard_ref,
    row_ref,
    act_ref,
    counts_ref,
    out_ref,
    edges_ref,
    mask_ref,
    table_vm,
    q_vm,
    rows_vm,
    kbuf,
    hgrad,
    wbuf,
    acc,
    pown,
    psend,
    psum,
    rsib,
    rgrad,
    load_sem,
    ksend,
    krecv,
    gsend,
    grecv,
    tsend,
    trecv,
):
    tok = k_ref.shape[0]
    width = k_ref.shape[1] // CHUNKS
    b = lax.axis_index("seq")
    core = lax.rem(b, 2)
    chip = lax.div(b, 2)
    chips = n // 2
    sib = b + 1 - 2 * core
    ahead = [chip + d < chips for d in range(1, REACH + 1)]
    behind = [chip >= d for d in range(1, REACH + 1)]
    last_ahead = chip + 4 * core < chips
    last_behind = chip >= 4 * (1 - core)
    last_key_to = b + 1 + 6 * core
    last_grad_to = b - 7 + 6 * core
    far = b - 7 + 14 * core
    has_far = jnp.logical_and(far >= 0, far < n)

    group = lax.axis_index("groups")
    lines = n // 4
    hi = lax.div(b, 4)
    lo = lax.rem(chip, 2)
    mine = core * 2 + lo
    half = table_hbm.shape[0] // 2
    part = pl.ds(pl.multiple_of(group * half, half), half)
    load_table = pltpu.make_async_copy(
        table_hbm.at[part], table_vm.at[mine, hi, part], load_sem.at[2]
    )
    load_table.start()
    load_q = pltpu.make_async_copy(q_hbm, q_vm, load_sem.at[0])
    load_rows = pltpu.make_async_copy(rows_hbm, rows_vm, load_sem.at[1])
    load_rows.start()
    load_q.start()

    barrier = pltpu.get_barrier_semaphore()
    partners = [(sib, None), (far, has_far)]
    for d in (1, 3):
        partners.append((b + 2 * d, ahead[d - 1]))
        partners.append((b - 2 * d, behind[d - 1]))

    def greet(device):
        pl.semaphore_signal(barrier, inc=1, device_id={"seq": device}, device_id_type=MESH)

    def on_line(o):
        return 4 * lax.rem(hi + o, lines) + 2 * lo + core

    for o in range(1, lines):
        greet(on_line(o))
    pl.semaphore_signal(barrier, inc=1, device_id={"groups": 1 - group}, device_id_type=MESH)

    for device, cond in partners:
        if cond is None:
            greet(device)
        else:
            pl.when(cond)(functools.partial(greet, device))
    peers = 1 + lines
    for _, cond in partners[1:]:
        peers = peers + jnp.where(cond, 1, 0)
    pl.semaphore_wait(barrier, peers)

    def cols(k):
        return pl.ds(pl.multiple_of(k * width, width), width)

    def remote(src, dst, send, recv, device):
        return pltpu.make_async_remote_copy(
            src_ref=src,
            dst_ref=dst,
            send_sem=send,
            recv_sem=recv,
            device_id={"seq": device},
            device_id_type=MESH,
        )

    def key_direct(d, k, device):
        return remote(
            k_ref.at[:, cols(k)], kbuf.at[d - 1, k], ksend.at[d - 1, k], krecv.at[d - 1, k], device
        )

    def key_share(d, k):
        i = REACH + d - 1
        return remote(kbuf.at[d - 1, k], kbuf.at[i, k], ksend.at[i, k], krecv.at[i, k], sib)

    def key_last(k, device):
        i = 2 * REACH
        return remote(k_ref.at[:, cols(k)], kbuf.at[i, k], ksend.at[i, k], krecv.at[i, k], device)

    def grad_share(d, k):
        return remote(
            psend.at[d - 1, k], rsib.at[d - 1, k], gsend.at[d - 1, k], grecv.at[d - 1, k], sib
        )

    def grad_direct(d, k, device):
        i = REACH + d - 1
        return remote(psum.at[d - 1, k], rgrad.at[d - 1, k], gsend.at[i, k], grecv.at[i, k], device)

    def grad_last(k, device):
        i = 2 * REACH
        return remote(
            psend.at[REACH, k], rgrad.at[REACH, k], gsend.at[i, k], grecv.at[i, k], device
        )

    def table_line(o):
        piece = table_vm.at[mine, hi, part]
        return remote(piece, piece, tsend.at[o - 1], trecv.at[o - 1], on_line(o))

    def table_lo():
        piece = table_vm.at[mine, :, part]
        i = lines - 1
        return remote(piece, piece, tsend.at[i], trecv.at[i], b + 2 - 4 * lo)

    def table_group():
        piece = table_vm.at[pl.ds(core * 2, 2), :, part]
        i = lines
        return pltpu.make_async_remote_copy(
            src_ref=piece,
            dst_ref=piece,
            send_sem=tsend.at[i],
            recv_sem=trecv.at[i],
            device_id={"groups": 1 - group},
            device_id_type=MESH,
        )

    def table_core():
        piece = table_vm.at[pl.ds(core * 2, 2)]
        i = lines + 1
        return remote(piece, piece, tsend.at[i], trecv.at[i], sib)

    def send_keys(chunks):
        for k in chunks:
            for d in range(1, REACH + 1):
                pl.when(ahead[d - 1])(lambda d=d, k=k: key_direct(d, k, b + 2 * d).start())
            pl.when(last_ahead)(lambda k=k: key_last(k, last_key_to).start())

    load_table.wait()
    for o in range(1, lines):
        table_line(o).start()
    send_keys(range(CHUNKS // 2))

    load_rows.wait()
    targets = rows_vm.shape[0]
    target = lax.broadcasted_iota(jnp.int32, (targets, tok), 0)
    spread = jnp.zeros((targets, tok), jnp.float32)
    for j in range(ids_ref.shape[0]):
        spread = spread + jnp.where(target == ids_ref[j : j + 1, :], weight_ref[j : j + 1, :], 0.0)
    spread = spread.T
    high = spread.astype(jnp.bfloat16)
    low = (spread - high.astype(jnp.float32)).astype(jnp.bfloat16)
    for g in range(KVH):
        columns = rows_vm[:, g * GROUP * HD : (g + 1) * GROUP * HD]
        grad = jnp.dot(high, columns, preferred_element_type=jnp.float32) + jnp.dot(
            low, columns, preferred_element_type=jnp.float32
        )
        grad = grad.astype(jnp.bfloat16)
        for h in range(GROUP):
            hgrad[g, h * tok : (h + 1) * tok, :] = grad[:, h * HD : (h + 1) * HD]
    for o in range(1, lines):
        table_line(o).wait_recv()
    table_lo().start()
    send_keys(range(CHUNKS // 2, CHUNKS))
    load_q.wait()

    def keeps(distance):
        return blocks_ref[0:1, distance - 1 : distance]

    for r in range(1, ROLES):
        if r <= REACH:
            kept, there = keeps(2 * r), behind[r - 1]
        elif r <= 2 * REACH:
            d = r - REACH
            kept = jnp.where(core == 0, keeps(2 * d - 1), keeps(2 * d + 1))
            there = behind[d - 1]
        else:
            kept, there = jnp.where(core == 0, keeps(WB - 1), keeps(1)), last_behind
        kept = jnp.where(there, kept, 0).astype(jnp.float32)
        mask_ref[r : r + 1, :] = jnp.broadcast_to(kept, (1, GROUP * tok))

    key_row = lax.broadcasted_iota(jnp.int32, (tok, GROUP * tok), 0)
    tok_col = lax.rem(lax.broadcasted_iota(jnp.int32, (tok, GROUP * tok), 1), tok)
    causal = key_row <= tok_col

    def tile_work(k):
        for gi in range(HEADS):
            head = slice(gi * HD, (gi + 1) * HD)
            pair = GROUP * HD
            offset = pl.multiple_of(k * (HEADS * pair) + gi * pair, pair)
            q = q_vm[:, pl.ds(offset, pair)]
            q2 = jnp.concatenate([q[:, h * HD : (h + 1) * HD] for h in range(GROUP)], axis=0)
            total = jnp.zeros((1, GROUP * tok), jnp.float32)
            for r in range(ROLES):
                if r == 0:
                    start = pl.multiple_of(k * width + gi * HD, HD)
                    key = k_ref[:, pl.ds(start, HD)]
                    keep = causal
                else:
                    key = kbuf[r - 1, k, :, head]
                    keep = mask_ref[r : r + 1, :] > 0.5
                score = lax.dot_general(
                    key, q2, (((1,), (1,)), ((), ())), preferred_element_type=jnp.float32
                )
                logit = (SOFTCAP * math.log2(math.e)) * jnp.tanh(
                    score * (QPRE ** (-0.5) / SOFTCAP)
                )
                w = jnp.exp2(jnp.where(keep, logit, -1.0e5))
                wbuf[r] = w
                total = total + jnp.sum(w, axis=0, keepdims=True)
            scale = 1.0 / total
            grad = hgrad[k * HEADS + gi]
            for r in range(ROLES):
                pattern = (wbuf[r] * scale).astype(jnp.bfloat16)
                grads = jnp.dot(pattern, grad, preferred_element_type=jnp.float32)
                if r == 0:
                    acc[k, :, head] = grads
                elif r <= REACH:
                    pown[r - 1, k, :, head] = grads
                else:
                    psend[r - 1 - REACH, k, :, head] = grads.astype(jnp.bfloat16)

    def reduce_pair(k):
        for d in range(1, REACH + 1):

            def one(d=d):
                grad_share(d, k).wait_recv()
                both = pown[d - 1, k] + rsib[d - 1, k].astype(jnp.float32)
                psum[d - 1, k] = both.astype(jnp.bfloat16)
                grad_direct(d, k, b - 2 * d).start()

            pl.when(behind[d - 1])(one)

    def chunk(k, carry):
        for d in range(1, REACH + 1):

            def share(d=d):
                key_direct(d, k, sib).wait_recv()
                key_share(d, k).start()

            pl.when(behind[d - 1])(share)
        for d in range(1, REACH + 1):
            pl.when(behind[d - 1])(lambda d=d: key_share(d, k).wait_recv())
        pl.when(last_behind)(lambda: key_last(k, sib).wait_recv())
        tile_work(k)
        for d in range(1, REACH + 1):
            pl.when(behind[d - 1])(lambda d=d: grad_share(d, k).start())
        pl.when(last_behind)(lambda: grad_last(k, last_grad_to).start())
        pl.when(k > 0)(lambda: reduce_pair(k - 1))

        def table_cross():
            table_lo().wait_recv()
            table_group().start()

        def table_share():
            table_group().wait_recv()
            table_core().start()

        pl.when(k == 0)(table_cross)
        pl.when(k == CHUNKS - 1)(table_share)
        return carry

    lax.fori_loop(0, CHUNKS, chunk, 0)
    reduce_pair(CHUNKS - 1)

    def finish(k, carry):
        for d in range(1, REACH + 1):

            def add(d=d):
                grad_direct(d, k, sib).wait_recv()
                acc[k] += rgrad[d - 1, k].astype(jnp.float32)

            pl.when(ahead[d - 1])(add)

        def add_last():
            grad_last(k, sib).wait_recv()
            acc[k] += rgrad[REACH, k].astype(jnp.float32)

        pl.when(last_ahead)(add_last)
        out_ref[:, cols(k)] = acc[k].astype(out_ref.dtype)
        return carry

    lax.fori_loop(0, CHUNKS, finish, 0)

    def drain(k, carry):
        for d in range(1, REACH + 1):
            pl.when(ahead[d - 1])(lambda d=d: key_direct(d, k, sib).wait_send())

            def back(d=d):
                key_share(d, k).wait_send()
                grad_share(d, k).wait_send()
                grad_direct(d, k, sib).wait_send()

            pl.when(behind[d - 1])(back)
        pl.when(last_ahead)(lambda: key_last(k, sib).wait_send())
        pl.when(last_behind)(lambda: grad_last(k, sib).wait_send())
        return carry

    lax.fori_loop(0, CHUNKS, drain, 0)


    table_core().wait_recv()
    shard = shard_ref[...]
    slot = (lax.rem(shard, 2) * 2 + lax.rem(lax.div(shard, 2), 2)) * lines + lax.div(shard, 4)
    depth = table_vm.shape[2]
    feature = slot * depth + row_ref[...]
    slots = feature.shape[0]
    some = math.gcd(lines, 4)
    step = some * depth
    place = lax.broadcasted_iota(jnp.int32, (step, tok), 0)
    vg = out_ref[...]

    def edge_step(i, found):
        per = lines // some
        rows = table_vm[lax.div(i, per), pl.ds(lax.rem(i, per) * some, some)].reshape(step, -1)
        product = lax.dot_general(
            rows, vg, (((1,), (1,)), ((), ())), preferred_element_type=jnp.float32
        )
        local = feature - i * step
        picked = [
            jnp.sum(jnp.where(place == local[a : a + 1, :], product, 0.0), axis=0, keepdims=True)
            for a in range(slots)
        ]
        return found + jnp.concatenate(picked, axis=0)

    found = lax.fori_loop(
        0, 4 * lines // some, edge_step, jnp.zeros((slots, tok), jnp.float32)
    )
    live = lax.broadcasted_iota(jnp.int32, (slots, tok), 0) < counts_ref[...]
    edges_ref[...] = jnp.where(live, act_ref[...] * found, 0.0)

    for o in range(1, lines):
        table_line(o).wait_send()
    table_lo().wait_send()
    table_group().wait_send()
    table_core().wait_send()


def body(
    queries,
    keys,
    target_rows,
    target_ids,
    target_weight,
    block_mask,
    value_table,
    feat_shard,
    feat_row,
    activation,
    counts,
):
    tok = queries.shape[0]
    kv_width = keys.shape[1]
    width = kv_width // CHUNKS
    slots = feat_shard.shape[1]
    n = lax.axis_size("seq")
    lines = n // 4

    vmem = pl.BlockSpec(memory_space=pltpu.VMEM)
    hbm = pl.BlockSpec(memory_space=pl.ANY)
    value_grad, edges = pl.pallas_call(
        functools.partial(attention_kernel, n),
        out_shape=(
            jax.ShapeDtypeStruct((tok, kv_width), jnp.bfloat16),
            jax.ShapeDtypeStruct((slots, tok), jnp.float32),
        ),
        in_specs=[hbm, vmem, hbm, vmem, vmem, vmem, hbm, vmem, vmem, vmem, vmem],
        out_specs=(vmem, vmem),
        scratch_shapes=[
            pltpu.VMEM((ROLES, GROUP * tok), jnp.float32),
            pltpu.VMEM((4, lines) + value_table.shape, jnp.bfloat16),
            pltpu.VMEM(queries.shape, jnp.bfloat16),
            pltpu.VMEM(target_rows.shape, jnp.bfloat16),
            pltpu.VMEM((ROLES - 1, CHUNKS, tok, width), jnp.bfloat16),
            pltpu.VMEM((KVH, GROUP * tok, HD), jnp.bfloat16),
            pltpu.VMEM((ROLES, tok, GROUP * tok), jnp.float32),
            pltpu.VMEM((CHUNKS, tok, width), jnp.float32),
            pltpu.VMEM((REACH, CHUNKS, tok, width), jnp.float32),
            pltpu.VMEM((REACH + 1, CHUNKS, tok, width), jnp.bfloat16),
            pltpu.VMEM((REACH, CHUNKS, tok, width), jnp.bfloat16),
            pltpu.VMEM((REACH, CHUNKS, tok, width), jnp.bfloat16),
            pltpu.VMEM((REACH + 1, CHUNKS, tok, width), jnp.bfloat16),
            pltpu.SemaphoreType.DMA((3,)),
            pltpu.SemaphoreType.DMA((ROLES - 1, CHUNKS)),
            pltpu.SemaphoreType.DMA((ROLES - 1, CHUNKS)),
            pltpu.SemaphoreType.DMA((ROLES - 1, CHUNKS)),
            pltpu.SemaphoreType.DMA((ROLES - 1, CHUNKS)),
            pltpu.SemaphoreType.DMA((lines + 2,)),
            pltpu.SemaphoreType.DMA((lines + 2,)),
        ],
        compiler_params=pltpu.CompilerParams(
            collective_id=0, has_side_effects=True, vmem_limit_bytes=VMEM_LIMIT
        ),
        cost_estimate=pl.CostEstimate(
            flops=2_000_000_000, bytes_accessed=100_000_000, transcendentals=4_000_000
        ),
        name="attention",
    )(
        queries,
        keys,
        target_rows,
        target_ids.T,
        target_weight.T,
        block_mask,
        value_table,
        feat_shard.T,
        feat_row.T,
        activation.T,
        counts[None, :],
    )
    return value_grad, edges.T


def solution(mesh):
    tokens = P(("groups", "seq"), None)
    in_specs = (
        tokens,
        tokens,
        P(),
        tokens,
        tokens,
        tokens,
        P("seq", None),
        tokens,
        tokens,
        tokens,
        P(("groups", "seq")),
    )
    return jax.shard_map(
        body, mesh=mesh, in_specs=in_specs, out_specs=(tokens, tokens), check_vma=False
    )
```

```python
import functools
import math

import jax
import jax.numpy as jnp
from jax import lax
from jax.experimental import pallas as pl
from jax.experimental.pallas import tpu as pltpu
from jax.sharding import PartitionSpec as P

H = 16
KVH = 8
HD = 128
QPRE = 144
WB = 8
FEAT_DEV = 64
SOFTCAP = 50.0

CHUNKS = 8
GROUP = H // KVH
HEADS = KVH // CHUNKS
REACH = (WB - 2) // 2
ROLES = WB
MESH = pl.DeviceIdType.MESH
VMEM_LIMIT = 60 * 1024 * 1024


def attention_kernel(
    n,
    q_hbm,
    k_ref,
    rows_hbm,
    ids_ref,
    weight_ref,
    blocks_ref,
    table_hbm,
    shard_ref,
    row_ref,
    act_ref,
    counts_ref,
    out_ref,
    edges_ref,
    mask_ref,
    table_vm,
    q_vm,
    rows_vm,
    kbuf,
    hgrad,
    wbuf,
    acc,
    pown,
    psend,
    psum,
    rsib,
    rgrad,
    load_sem,
    ksend,
    krecv,
    gsend,
    grecv,
    tsend,
    trecv,
):
    tok = k_ref.shape[0]
    width = k_ref.shape[1] // CHUNKS
    b = lax.axis_index("seq")
    core = lax.rem(b, 2)
    chip = lax.div(b, 2)
    chips = n // 2
    sib = b + 1 - 2 * core
    ahead = [chip + d < chips for d in range(1, REACH + 1)]
    behind = [chip >= d for d in range(1, REACH + 1)]
    last_ahead = chip + 4 * core < chips
    last_behind = chip >= 4 * (1 - core)
    last_key_to = b + 1 + 6 * core
    last_grad_to = b - 7 + 6 * core
    far = b - 7 + 14 * core
    has_far = jnp.logical_and(far >= 0, far < n)

    group = lax.axis_index("groups")
    lines = n // 4
    hi = lax.div(b, 4)
    lo = lax.rem(chip, 2)
    mine = core * 2 + lo
    half = table_hbm.shape[0] // 2
    part = pl.ds(pl.multiple_of(group * half, half), half)
    load_table = pltpu.make_async_copy(
        table_hbm.at[part], table_vm.at[mine, hi, part], load_sem.at[2]
    )
    load_table.start()
    load_q = pltpu.make_async_copy(q_hbm, q_vm, load_sem.at[0])
    load_rows = pltpu.make_async_copy(rows_hbm, rows_vm, load_sem.at[1])
    load_rows.start()
    load_q.start()

    barrier = pltpu.get_barrier_semaphore()
    partners = [(sib, None), (far, has_far)]
    for d in (1, 3):
        partners.append((b + 2 * d, ahead[d - 1]))
        partners.append((b - 2 * d, behind[d - 1]))

    def greet(device):
        pl.semaphore_signal(barrier, inc=1, device_id={"seq": device}, device_id_type=MESH)

    def on_line(o):
        return 4 * lax.rem(hi + o, lines) + 2 * lo + core

    for o in range(1, lines):
        greet(on_line(o))
    pl.semaphore_signal(barrier, inc=1, device_id={"groups": 1 - group}, device_id_type=MESH)

    for device, cond in partners:
        if cond is None:
            greet(device)
        else:
            pl.when(cond)(functools.partial(greet, device))
    peers = 1 + lines
    for _, cond in partners[1:]:
        peers = peers + jnp.where(cond, 1, 0)
    pl.semaphore_wait(barrier, peers)

    def cols(k):
        return pl.ds(pl.multiple_of(k * width, width), width)

    def remote(src, dst, send, recv, device):
        return pltpu.make_async_remote_copy(
            src_ref=src,
            dst_ref=dst,
            send_sem=send,
            recv_sem=recv,
            device_id={"seq": device},
            device_id_type=MESH,
        )

    def key_direct(d, k, device):
        return remote(
            k_ref.at[:, cols(k)], kbuf.at[d - 1, k], ksend.at[d - 1, k], krecv.at[d - 1, k], device
        )

    def key_share(d, k):
        i = REACH + d - 1
        return remote(kbuf.at[d - 1, k], kbuf.at[i, k], ksend.at[i, k], krecv.at[i, k], sib)

    def key_last(k, device):
        i = 2 * REACH
        return remote(k_ref.at[:, cols(k)], kbuf.at[i, k], ksend.at[i, k], krecv.at[i, k], device)

    def grad_share(d, k):
        return remote(
            psend.at[d - 1, k], rsib.at[d - 1, k], gsend.at[d - 1, k], grecv.at[d - 1, k], sib
        )

    def grad_direct(d, k, device):
        i = REACH + d - 1
        return remote(psum.at[d - 1, k], rgrad.at[d - 1, k], gsend.at[i, k], grecv.at[i, k], device)

    def grad_last(k, device):
        i = 2 * REACH
        return remote(
            psend.at[REACH, k], rgrad.at[REACH, k], gsend.at[i, k], grecv.at[i, k], device
        )

    def table_line(o):
        piece = table_vm.at[mine, hi, part]
        return remote(piece, piece, tsend.at[o - 1], trecv.at[o - 1], on_line(o))

    def table_lo():
        piece = table_vm.at[mine, :, part]
        i = lines - 1
        return remote(piece, piece, tsend.at[i], trecv.at[i], b + 2 - 4 * lo)

    def table_group():
        piece = table_vm.at[pl.ds(core * 2, 2), :, part]
        i = lines
        return pltpu.make_async_remote_copy(
            src_ref=piece,
            dst_ref=piece,
            send_sem=tsend.at[i],
            recv_sem=trecv.at[i],
            device_id={"groups": 1 - group},
            device_id_type=MESH,
        )

    def table_core():
        piece = table_vm.at[pl.ds(core * 2, 2)]
        i = lines + 1
        return remote(piece, piece, tsend.at[i], trecv.at[i], sib)

    def send_keys(chunks):
        for k in chunks:
            for d in range(1, REACH + 1):
                pl.when(ahead[d - 1])(lambda d=d, k=k: key_direct(d, k, b + 2 * d).start())
            pl.when(last_ahead)(lambda k=k: key_last(k, last_key_to).start())

    load_table.wait()
    for o in range(1, lines):
        table_line(o).start()
    send_keys(range(CHUNKS // 2))

    load_rows.wait()
    targets = rows_vm.shape[0]
    target = lax.broadcasted_iota(jnp.int32, (targets, tok), 0)
    spread = jnp.zeros((targets, tok), jnp.float32)
    for j in range(ids_ref.shape[0]):
        spread = spread + jnp.where(target == ids_ref[j : j + 1, :], weight_ref[j : j + 1, :], 0.0)
    spread = spread.T
    high = spread.astype(jnp.bfloat16)
    low = (spread - high.astype(jnp.float32)).astype(jnp.bfloat16)
    for g in range(KVH):
        columns = rows_vm[:, g * GROUP * HD : (g + 1) * GROUP * HD]
        grad = jnp.dot(high, columns, preferred_element_type=jnp.float32) + jnp.dot(
            low, columns, preferred_element_type=jnp.float32
        )
        grad = grad.astype(jnp.bfloat16)
        for h in range(GROUP):
            hgrad[g, h * tok : (h + 1) * tok, :] = grad[:, h * HD : (h + 1) * HD]
    for o in range(1, lines):
        table_line(o).wait_recv()
    table_lo().start()
    send_keys(range(CHUNKS // 2, CHUNKS))
    load_q.wait()

    def keeps(distance):
        return blocks_ref[0:1, distance - 1 : distance]

    for r in range(1, ROLES):
        if r <= REACH:
            kept, there = keeps(2 * r), behind[r - 1]
        elif r <= 2 * REACH:
            d = r - REACH
            kept = jnp.where(core == 0, keeps(2 * d - 1), keeps(2 * d + 1))
            there = behind[d - 1]
        else:
            kept, there = jnp.where(core == 0, keeps(WB - 1), keeps(1)), last_behind
        kept = jnp.where(there, kept, 0).astype(jnp.float32)
        mask_ref[r : r + 1, :] = jnp.broadcast_to(kept, (1, GROUP * tok))

    key_row = lax.broadcasted_iota(jnp.int32, (tok, GROUP * tok), 0)
    tok_col = lax.rem(lax.broadcasted_iota(jnp.int32, (tok, GROUP * tok), 1), tok)
    causal = key_row <= tok_col

    def tile_work(k):
        for gi in range(HEADS):
            head = slice(gi * HD, (gi + 1) * HD)
            pair = GROUP * HD
            offset = pl.multiple_of(k * (HEADS * pair) + gi * pair, pair)
            q = q_vm[:, pl.ds(offset, pair)]
            q2 = jnp.concatenate([q[:, h * HD : (h + 1) * HD] for h in range(GROUP)], axis=0)
            total = jnp.zeros((1, GROUP * tok), jnp.float32)
            for r in range(ROLES):
                if r == 0:
                    start = pl.multiple_of(k * width + gi * HD, HD)
                    key = k_ref[:, pl.ds(start, HD)]
                    keep = causal
                else:
                    key = kbuf[r - 1, k, :, head]
                    keep = mask_ref[r : r + 1, :] > 0.5
                score = lax.dot_general(
                    key, q2, (((1,), (1,)), ((), ())), preferred_element_type=jnp.float32
                )
                logit = (SOFTCAP * math.log2(math.e)) * jnp.tanh(
                    score * (QPRE ** (-0.5) / SOFTCAP)
                )
                w = jnp.exp2(jnp.where(keep, logit, -1.0e5))
                wbuf[r] = w
                total = total + jnp.sum(w, axis=0, keepdims=True)
            scale = 1.0 / total
            grad = hgrad[k * HEADS + gi]
            for r in range(ROLES):
                pattern = (wbuf[r] * scale).astype(jnp.bfloat16)
                grads = jnp.dot(pattern, grad, preferred_element_type=jnp.float32)
                if r == 0:
                    acc[k, :, head] = grads
                elif r <= REACH:
                    pown[r - 1, k, :, head] = grads
                else:
                    psend[r - 1 - REACH, k, :, head] = grads.astype(jnp.bfloat16)

    def reduce_pair(k):
        for d in range(1, REACH + 1):

            def one(d=d):
                grad_share(d, k).wait_recv()
                both = pown[d - 1, k] + rsib[d - 1, k].astype(jnp.float32)
                psum[d - 1, k] = both.astype(jnp.bfloat16)
                grad_direct(d, k, b - 2 * d).start()

            pl.when(behind[d - 1])(one)

    def chunk(k, carry):
        for d in range(1, REACH + 1):

            def share(d=d):
                key_direct(d, k, sib).wait_recv()
                key_share(d, k).start()

            pl.when(behind[d - 1])(share)
        for d in range(1, REACH + 1):
            pl.when(behind[d - 1])(lambda d=d: key_share(d, k).wait_recv())
        pl.when(last_behind)(lambda: key_last(k, sib).wait_recv())
        tile_work(k)
        for d in range(1, REACH + 1):
            pl.when(behind[d - 1])(lambda d=d: grad_share(d, k).start())
        pl.when(last_behind)(lambda: grad_last(k, last_grad_to).start())
        pl.when(k > 0)(lambda: reduce_pair(k - 1))

        def table_cross():
            table_lo().wait_recv()
            table_group().start()

        def table_share():
            table_group().wait_recv()
            table_core().start()

        pl.when(k == 0)(table_cross)
        pl.when(k == CHUNKS - 1)(table_share)
        return carry

    lax.fori_loop(0, CHUNKS, chunk, 0)
    reduce_pair(CHUNKS - 1)

    def finish(k, carry):
        for d in range(1, REACH + 1):

            def add(d=d):
                grad_direct(d, k, sib).wait_recv()
                acc[k] += rgrad[d - 1, k].astype(jnp.float32)

            pl.when(ahead[d - 1])(add)

        def add_last():
            grad_last(k, sib).wait_recv()
            acc[k] += rgrad[REACH, k].astype(jnp.float32)

        pl.when(last_ahead)(add_last)
        out_ref[:, cols(k)] = acc[k].astype(out_ref.dtype)
        return carry

    lax.fori_loop(0, CHUNKS, finish, 0)

    def drain(k, carry):
        for d in range(1, REACH + 1):
            pl.when(ahead[d - 1])(lambda d=d: key_direct(d, k, sib).wait_send())

            def back(d=d):
                key_share(d, k).wait_send()
                grad_share(d, k).wait_send()
                grad_direct(d, k, sib).wait_send()

            pl.when(behind[d - 1])(back)
        pl.when(last_ahead)(lambda: key_last(k, sib).wait_send())
        pl.when(last_behind)(lambda: grad_last(k, sib).wait_send())
        return carry

    lax.fori_loop(0, CHUNKS, drain, 0)


    table_core().wait_recv()
    shard = shard_ref[...]
    slot = (lax.rem(shard, 2) * 2 + lax.rem(lax.div(shard, 2), 2)) * lines + lax.div(shard, 4)
    depth = table_vm.shape[2]
    feature = slot * depth + row_ref[...]
    slots = feature.shape[0]
    some = math.gcd(lines, 4)
    step = some * depth
    place = lax.broadcasted_iota(jnp.int32, (step, tok), 0)
    vg = out_ref[...]

    def edge_step(i, found):
        per = lines // some
        rows = table_vm[lax.div(i, per), pl.ds(lax.rem(i, per) * some, some)].reshape(step, -1)
        product = lax.dot_general(
            rows, vg, (((1,), (1,)), ((), ())), preferred_element_type=jnp.float32
        )
        local = feature - i * step
        picked = [
            jnp.sum(jnp.where(place == local[a : a + 1, :], product, 0.0), axis=0, keepdims=True)
            for a in range(slots)
        ]
        return found + jnp.concatenate(picked, axis=0)

    found = lax.fori_loop(
        0, 4 * lines // some, edge_step, jnp.zeros((slots, tok), jnp.float32)
    )
    live = lax.broadcasted_iota(jnp.int32, (slots, tok), 0) < counts_ref[...]
    edges_ref[...] = jnp.where(live, act_ref[...] * found, 0.0)

    for o in range(1, lines):
        table_line(o).wait_send()
    table_lo().wait_send()
    table_group().wait_send()
    table_core().wait_send()


def body(
    queries,
    keys,
    target_rows,
    target_ids,
    target_weight,
    block_mask,
    value_table,
    feat_shard,
    feat_row,
    activation,
    counts,
):
    tok = queries.shape[0]
    kv_width = keys.shape[1]
    width = kv_width // CHUNKS
    slots = feat_shard.shape[1]
    n = lax.axis_size("seq")
    lines = n // 4

    vmem = pl.BlockSpec(memory_space=pltpu.VMEM)
    hbm = pl.BlockSpec(memory_space=pl.ANY)
    value_grad, edges = pl.pallas_call(
        functools.partial(attention_kernel, n),
        out_shape=(
            jax.ShapeDtypeStruct((tok, kv_width), jnp.bfloat16),
            jax.ShapeDtypeStruct((slots, tok), jnp.float32),
        ),
        in_specs=[hbm, vmem, hbm, vmem, vmem, vmem, hbm, vmem, vmem, vmem, vmem],
        out_specs=(vmem, vmem),
        scratch_shapes=[
            pltpu.VMEM((ROLES, GROUP * tok), jnp.float32),
            pltpu.VMEM((4, lines) + value_table.shape, jnp.bfloat16),
            pltpu.VMEM(queries.shape, jnp.bfloat16),
            pltpu.VMEM(target_rows.shape, jnp.bfloat16),
            pltpu.VMEM((ROLES - 1, CHUNKS, tok, width), jnp.bfloat16),
            pltpu.VMEM((KVH, GROUP * tok, HD), jnp.bfloat16),
            pltpu.VMEM((ROLES, tok, GROUP * tok), jnp.float32),
            pltpu.VMEM((CHUNKS, tok, width), jnp.float32),
            pltpu.VMEM((REACH, CHUNKS, tok, width), jnp.float32),
            pltpu.VMEM((REACH + 1, CHUNKS, tok, width), jnp.bfloat16),
            pltpu.VMEM((REACH, CHUNKS, tok, width), jnp.bfloat16),
            pltpu.VMEM((REACH, CHUNKS, tok, width), jnp.bfloat16),
            pltpu.VMEM((REACH + 1, CHUNKS, tok, width), jnp.bfloat16),
            pltpu.SemaphoreType.DMA((3,)),
            pltpu.SemaphoreType.DMA((ROLES - 1, CHUNKS)),
            pltpu.SemaphoreType.DMA((ROLES - 1, CHUNKS)),
            pltpu.SemaphoreType.DMA((ROLES - 1, CHUNKS)),
            pltpu.SemaphoreType.DMA((ROLES - 1, CHUNKS)),
            pltpu.SemaphoreType.DMA((lines + 2,)),
            pltpu.SemaphoreType.DMA((lines + 2,)),
        ],
        compiler_params=pltpu.CompilerParams(
            collective_id=0, has_side_effects=True, vmem_limit_bytes=VMEM_LIMIT
        ),
        cost_estimate=pl.CostEstimate(
            flops=2_000_000_000, bytes_accessed=100_000_000, transcendentals=4_000_000
        ),
        name="attention",
    )(
        queries,
        keys,
        target_rows,
        target_ids.T,
        target_weight.T,
        block_mask,
        value_table,
        feat_shard.T,
        feat_row.T,
        activation.T,
        counts[None, :],
    )
    return value_grad, edges.T


def solution(mesh):
    tokens = P(("groups", "seq"), None)
    in_specs = (
        tokens,
        tokens,
        P(),
        tokens,
        tokens,
        tokens,
        P("seq", None),
        tokens,
        tokens,
        tokens,
        P(("groups", "seq")),
    )
    return jax.shard_map(
        body, mesh=mesh, in_specs=in_specs, out_specs=(tokens, tokens), check_vma=False
    )
```
